1024 devices in a mesh: dp: 8 (over x), fsdp: 128 (over z, y, core).
Axes of the slice: x: 8, y: 8, z: 8, core: 2. Of those that a mesh axis runs over, the one named last changes fastest.
Arguments:
- acts: bfloat16 [16384, 8192], P('fsdp', 'dp'), may hold values from -6 to 6
- out_grad: bfloat16 [16384, 28672], P(None, 'fsdp'), may hold values from -0.09375 to 0.09375
- basis: bfloat16 [8192, 512], P('dp'), may hold values from -0.0625 to 0.0625
- first_moment: float32 [512, 28672], P('dp', 'fsdp'), may hold values from -6 to 6
- second_moment: float32 [512, 28672], P('dp', 'fsdp'), may hold values from 0.01 to 1
Outputs:
- update: float32 [8192, 28672], P('dp', 'fsdp')
- new_first: float32 [512, 28672], P('dp', 'fsdp')
- new_second: float32 [512, 28672], P('dp', 'fsdp')
The draws below stay inside these ranges and needn't reach their ends.
All inputs are finite; a program needn't handle non-finite values.
Results may differ from the reference program's by a relative error of at most 0.0029.
Values may be sent and summed in bfloat16 or wider, within the bound.
No kernel may reach another device: no remote copies, remote signals or barrier semaphores. Data moves between devices by JAX's collectives and lax.ppermute only.
A program may use at most 128 MiB of HBM per device.

```python
import math
import jax
import jax.numpy as jnp
from jax import lax

D = 8192
FF = 28672
RANK = 512
STEP = 1000
TOKENS = 16384


def shard_levels(rng, shape, shards, smallest, high):
    loudness = 1.0
    for axis_at, blocks in shards:
        draws = jax.random.uniform(jax.random.fold_in(jax.random.fold_in(rng, 6), axis_at), (blocks,), jnp.float32, smallest / len(shards), high / len(shards))
        loudness = loudness * jnp.repeat(jnp.exp(draws), shape[axis_at] // blocks).reshape((-1,) + (1,) * (len(shape) - 1 - axis_at))
    return loudness


def noise(stream_key, extent, deviation, bound, cuts=(), held_as=jnp.bfloat16):
    entries = jax.random.normal(stream_key, extent, jnp.float32) * deviation
    if len(cuts) > 0:
        entries = shard_levels(stream_key, extent, cuts, -0.22, 0.18) * entries
    return jnp.clip(entries, min=-bound, max=bound).astype(held_as)


def setup_inputs(seed: int = 0) -> dict:
    keys = jax.random.split(jax.random.key(seed), 6)
    acts = noise(keys[0], (TOKENS, D), 1.0, 6.0, ((0, 128), (1, 8)))
    out_grad = noise(keys[1], (TOKENS, FF), (2.0 * TOKENS ** -0.5), 0.09375, ((1, 128),))
    basis = noise(keys[2], (D, RANK), D ** -0.5, 0.0625, ((0, 8),))
    first_moment = noise(keys[3], (RANK, FF), 1.0, 6.0, ((0, 8), (1, 128)), jnp.float32)
    second_moment = jnp.clip(jnp.exp(math.log(1.0) - 4.6051702 * jax.random.uniform(keys[4], (RANK, FF), jnp.float32) ** shard_levels(keys[4], (RANK, FF), ((0, 8), (1, 128)), -0.2, 0.2)), 0.01, 1.0)
    return dict(acts=acts, out_grad=out_grad, basis=basis, first_moment=first_moment, second_moment=second_moment)


beta_first = 0.9
beta_second = 0.999
adam_epsilon = 1e-08

def moments_step(grad_low, first_moment, second_moment):
    new_first = beta_first * first_moment + (1.0 - beta_first) * grad_low
    new_second = beta_second * second_moment + (1.0 - beta_second) * grad_low * grad_low
    corrected_first = new_first / (1.0 - beta_first ** STEP)
    corrected_second = new_second / (1.0 - beta_second ** STEP)
    direction = (corrected_first / (jnp.sqrt(corrected_second) + adam_epsilon)).astype(jnp.bfloat16)
    return (new_first, new_second, direction)

def reference(acts, out_grad, basis, first_moment, second_moment):
    projected = jnp.dot(acts, basis, preferred_element_type=jnp.float32)
    grad_low = lax.dot_general(projected, out_grad.astype(jnp.float32), (((0,), (0,)), ((), ())), precision=lax.Precision.HIGHEST, preferred_element_type=jnp.float32)
    new_first, new_second, direction = moments_step(grad_low, first_moment, second_moment)
    update = jnp.dot(basis, direction, preferred_element_type=jnp.float32)
    return (update, new_first, new_second)
```

```python
import functools

import jax
import jax.numpy as jnp
import numpy as np
from jax import lax
from jax.experimental import pallas as pl
from jax.experimental.pallas import tpu as pltpu
from jax.sharding import Mesh
from jax.sharding import PartitionSpec as P

STEP = 1000


beta_first = 0.9
beta_second = 0.999
adam_epsilon = 1e-08


def moments_step(grad_low, first_moment, second_moment):
    new_first = beta_first * first_moment + (1.0 - beta_first) * grad_low
    new_second = beta_second * second_moment + (1.0 - beta_second) * grad_low * grad_low
    corrected_first = new_first / (1.0 - beta_first**STEP)
    corrected_second = new_second / (1.0 - beta_second**STEP)
    direction = (corrected_first / (jnp.sqrt(corrected_second) + adam_epsilon)).astype(jnp.bfloat16)
    return (new_first, new_second, direction)


def grad_kernel(steps, core_ref, own_ref, other_ref, grad_t_ref, first_ref, second_ref,
                new_first_ref, new_second_ref, spread_ref, total_ref):
    step = pl.program_id(0)

    @pl.when(step == 0)
    def _():
        total_ref[...] = jnp.zeros_like(total_ref)

    is_first = core_ref[0] == 0
    chips = own_ref.shape[0]
    pieces = []
    for chip in range(chips):
        own, other = own_ref[chip], other_ref[chip]
        pieces += [jnp.where(is_first, own, other), jnp.where(is_first, other, own)]
    projected = jnp.concatenate(pieces, axis=1)
    total_ref[...] += lax.dot_general(
        projected, grad_t_ref[...], (((1,), (1,)), ((), ())), preferred_element_type=jnp.float32
    )

    @pl.when(step == steps - 1)
    def _():
        new_first, new_second, direction = moments_step(total_ref[...], first_ref[...], second_ref[...])
        new_first_ref[...] = new_first
        new_second_ref[...] = new_second
        for copy in range(spread_ref.shape[0]):
            spread_ref[copy] = direction


def grad_and_moments(core, own, other, grad_t, first_moment, second_moment, copies):
    chips, rank, rows = own.shape
    hidden, tokens = grad_t.shape
    steps = 8
    whole = lambda shape: pl.BlockSpec(shape, lambda s, c: (0,) * len(shape))
    return pl.pallas_call(
        functools.partial(grad_kernel, steps),
        grid_spec=pltpu.PrefetchScalarGridSpec(
            num_scalar_prefetch=1,
            grid=(steps,),
            in_specs=[
                pl.BlockSpec((chips // steps, rank, rows), lambda s, c: (s, 0, 0)),
                pl.BlockSpec((chips // steps, rank, rows), lambda s, c: (s, 0, 0)),
                pl.BlockSpec((hidden, tokens // steps), lambda s, c: (0, s)),
                whole((rank, hidden)),
                whole((rank, hidden)),
            ],
            out_specs=[whole((rank, hidden)), whole((rank, hidden)), whole((copies, rank, hidden))],
            scratch_shapes=[pltpu.VMEM((rank, hidden), jnp.float32)],
        ),
        out_shape=[
            jax.ShapeDtypeStruct((rank, hidden), jnp.float32),
            jax.ShapeDtypeStruct((rank, hidden), jnp.float32),
            jax.ShapeDtypeStruct((copies, rank, hidden), jnp.bfloat16),
        ],
        compiler_params=pltpu.CompilerParams(vmem_limit_bytes=32 * 1024 * 1024),
        cost_estimate=pl.CostEstimate(
            flops=2 * rank * hidden * tokens,
            bytes_accessed=2 * (hidden * tokens + rank * tokens),
            transcendentals=rank * hidden,
        ),
    )(core, own, other, grad_t, first_moment, second_moment)


def per_device(acts, out_grad, basis, first_moment, second_moment):
    splits = lax.axis_size("x")
    chips = lax.axis_size("z") * lax.axis_size("y")
    tokens = acts.shape[0]
    rank = basis.shape[1] // splits
    local_terms = lax.dot_general(
        basis, acts, (((0,), (1,)), ((), ())), preferred_element_type=jnp.float32
    ).astype(jnp.bfloat16)
    terms = lax.all_to_all(
        local_terms.reshape(splits, rank, tokens), "x", split_axis=0, concat_axis=0, tiled=True
    )
    share = jnp.sum(terms.astype(jnp.float32), axis=0).astype(jnp.bfloat16)
    spread = jnp.broadcast_to(share[None], (chips, rank, tokens))
    own = lax.all_to_all(spread, ("z", "y"), split_axis=0, concat_axis=0, tiled=True)
    other = lax.ppermute(own, "c", [(0, 1), (1, 0)])
    core = lax.axis_index("c").astype(jnp.int32).reshape(1)
    new_first, new_second, direction = grad_and_moments(
        core, own, other, out_grad.T, first_moment, second_moment, splits
    )
    pieces = lax.all_to_all(direction, "x", split_axis=0, concat_axis=0, tiled=True)
    piece = pieces.reshape(splits * rank, pieces.shape[2])
    update = jnp.dot(basis, piece, preferred_element_type=jnp.float32)
    return (update, new_first, new_second)


def solution(mesh):
    chips = Mesh(np.asarray(mesh.devices).reshape(8, 8, 8, 2), ("x", "z", "y", "c"))
    fsdp = ("z", "y", "c")
    return jax.shard_map(
        per_device,
        mesh=chips,
        in_specs=(P(fsdp, "x"), P(None, fsdp), P("x", None), P("x", fsdp), P("x", fsdp)),
        out_specs=(P("x", fsdp), P("x", fsdp), P("x", fsdp)),
        check_vma=False,
    )
```

```python
import jax
import jax.numpy as jnp
import numpy as np
from jax import lax
from jax.experimental import pallas as pl
from jax.experimental.pallas import tpu as pltpu
from jax.sharding import Mesh
from jax.sharding import PartitionSpec as P

STEP = 1000


beta_first = 0.9
beta_second = 0.999
adam_epsilon = 1e-08


def moments_step(grad_low, first_moment, second_moment):
    new_first = beta_first * first_moment + (1.0 - beta_first) * grad_low
    new_second = beta_second * second_moment + (1.0 - beta_second) * grad_low * grad_low
    corrected_first = new_first / (1.0 - beta_first**STEP)
    corrected_second = new_second / (1.0 - beta_second**STEP)
    direction = (corrected_first / (jnp.sqrt(corrected_second) + adam_epsilon)).astype(jnp.bfloat16)
    return (new_first, new_second, direction)


CHUNKS = 8


def spread_kernel(terms_ref, spread_ref):
    total = terms_ref[0].astype(jnp.float32)
    for split in range(1, terms_ref.shape[0]):
        total += terms_ref[split].astype(jnp.float32)
    share = total.astype(jnp.bfloat16)

    @pl.loop(0, spread_ref.shape[0])
    def _(chip):
        spread_ref[chip] = share


def sum_and_spread(terms, copies):
    return pl.pallas_call(
        spread_kernel,
        in_specs=[pl.BlockSpec(memory_space=pltpu.VMEM)],
        out_specs=pl.BlockSpec(memory_space=pltpu.VMEM),
        out_shape=jax.ShapeDtypeStruct((copies,) + terms.shape[1:], jnp.bfloat16),
        compiler_params=pltpu.CompilerParams(vmem_limit_bytes=8 * 1024 * 1024),
    )(terms)


def half_dot(side, projected_ref, grad_t_ref, first_chip, chips):
    rows = projected_ref.shape[2]
    at = lambda chip: pl.ds(pl.multiple_of((2 * chip + side) * rows, rows), rows)
    members = range(first_chip, first_chip + chips)
    projected = jnp.concatenate([projected_ref[chip] for chip in members], axis=1)
    grad_t = jnp.concatenate([grad_t_ref[:, at(chip)] for chip in members], axis=1)
    return lax.dot_general(
        grad_t, projected, (((1,), (1,)), ((), ())), preferred_element_type=jnp.float32
    )


def own_kernel(core_ref, own_ref, grad_t_ref, held_ref, partial_ref, sems):
    tokens = grad_t_ref.shape[1] // CHUNKS
    chips = own_ref.shape[0] // CHUNKS
    copies = []
    for chunk in range(CHUNKS):
        part = pl.ds(chunk * tokens, tokens)
        copies.append(
            pltpu.make_async_copy(grad_t_ref.at[:, part], held_ref.at[:, part], sems.at[chunk])
        )
        copies[-1].start()
    total = jnp.zeros(partial_ref.shape, jnp.float32)
    for chunk in range(CHUNKS):
        copies[chunk].wait()
        total += half_dot(core_ref[0], own_ref, held_ref, chunk * chips, chips)
    partial_ref[...] = total


def own_half(core, own, grad_t):
    chips, rank, rows = own.shape
    hidden, tokens = grad_t.shape
    return pl.pallas_call(
        own_kernel,
        in_specs=[
            pl.BlockSpec(memory_space=pltpu.SMEM),
            pl.BlockSpec(memory_space=pltpu.VMEM),
            pl.BlockSpec(memory_space=pltpu.HBM),
        ],
        out_specs=[pl.BlockSpec(memory_space=pltpu.VMEM), pl.BlockSpec(memory_space=pltpu.VMEM)],
        out_shape=[
            jax.ShapeDtypeStruct((hidden, tokens), jnp.bfloat16),
            jax.ShapeDtypeStruct((hidden, rank), jnp.float32),
        ],
        scratch_shapes=[pltpu.SemaphoreType.DMA((CHUNKS,))],
        compiler_params=pltpu.CompilerParams(vmem_limit_bytes=24 * 1024 * 1024),
        cost_estimate=pl.CostEstimate(
            flops=2 * rank * hidden * tokens, bytes_accessed=4 * hidden * tokens, transcendentals=0
        ),
    )(core, own, grad_t)


def moments_kernel(core_ref, other_ref, held_ref, partial_ref, first_ref, second_ref,
                   new_first_ref, new_second_ref, spread_ref, first_in, second_in, sems):
    reads = [
        pltpu.make_async_copy(first_ref, first_in, sems.at[0]),
        pltpu.make_async_copy(second_ref, second_in, sems.at[1]),
    ]
    for read in reads:
        read.start()
    chips = other_ref.shape[0] // CHUNKS
    total = partial_ref[...]
    for chunk in range(CHUNKS):
        total += half_dot(1 - core_ref[0], other_ref, held_ref, chunk * chips, chips)
    for read in reads:
        read.wait()
    new_first, new_second, direction = moments_step(total.T, first_in[...], second_in[...])
    new_first_ref[...] = new_first
    new_second_ref[...] = new_second
    for copy in range(spread_ref.shape[0]):
        spread_ref[copy] = direction


def other_half_and_moments(core, other, held, partial, first_moment, second_moment, copies):
    rank, hidden = first_moment.shape
    vmem = pl.BlockSpec(memory_space=pltpu.VMEM)
    hbm = pl.BlockSpec(memory_space=pltpu.HBM)
    return pl.pallas_call(
        moments_kernel,
        in_specs=[pl.BlockSpec(memory_space=pltpu.SMEM), vmem, vmem, vmem, hbm, hbm],
        out_specs=[vmem, vmem, vmem],
        out_shape=[
            jax.ShapeDtypeStruct((rank, hidden), jnp.float32),
            jax.ShapeDtypeStruct((rank, hidden), jnp.float32),
            jax.ShapeDtypeStruct((copies, rank, hidden), jnp.bfloat16),
        ],
        scratch_shapes=[
            pltpu.VMEM((rank, hidden), jnp.float32),
            pltpu.VMEM((rank, hidden), jnp.float32),
            pltpu.SemaphoreType.DMA((2,)),
        ],
        compiler_params=pltpu.CompilerParams(vmem_limit_bytes=24 * 1024 * 1024),
    )(core, other, held, partial, first_moment, second_moment)


def per_device(acts, out_grad, basis, first_moment, second_moment):
    splits = lax.axis_size("x")
    chips = lax.axis_size("z") * lax.axis_size("y")
    tokens = acts.shape[0]
    rank = basis.shape[1] // splits
    local_terms = lax.dot_general(
        basis, acts, (((0,), (1,)), ((), ())), preferred_element_type=jnp.float32
    ).astype(jnp.bfloat16)
    terms = lax.all_to_all(
        local_terms.reshape(splits, rank, tokens), "x", split_axis=0, concat_axis=0, tiled=True
    )
    spread = sum_and_spread(terms, chips)
    own = lax.all_to_all(spread, ("z", "y"), split_axis=0, concat_axis=0, tiled=True)
    other = lax.ppermute(own, "c", [(0, 1), (1, 0)])
    core = lax.axis_index("c").astype(jnp.int32).reshape(1)
    held, partial = own_half(core, own, pltpu.with_memory_space_constraint(out_grad.T, pltpu.HBM))
    new_first, new_second, direction = other_half_and_moments(
        core, other, held, partial, first_moment, second_moment, splits
    )
    pieces = lax.all_to_all(direction, "x", split_axis=0, concat_axis=0, tiled=True)
    piece = pieces.reshape(splits * rank, pieces.shape[2])
    update = jnp.dot(basis, piece, preferred_element_type=jnp.float32)
    return (update, new_first, new_second)


def solution(mesh):
    chips = Mesh(np.asarray(mesh.devices).reshape(8, 8, 8, 2), ("x", "z", "y", "c"))
    fsdp = ("z", "y", "c")
    return jax.shard_map(
        per_device,
        mesh=chips,
        in_specs=(P(fsdp, "x"), P(None, fsdp), P("x", None), P("x", fsdp), P("x", fsdp)),
        out_specs=(P("x", fsdp), P("x", fsdp), P("x", fsdp)),
        check_vma=False,
    )
```

```python
import jax
import jax.numpy as jnp
import numpy as np
from jax import lax
from jax.experimental import pallas as pl
from jax.experimental.pallas import tpu as pltpu
from jax.sharding import Mesh
from jax.sharding import PartitionSpec as P

STEP = 1000


beta_first = 0.9
beta_second = 0.999
adam_epsilon = 1e-08


def moments_step(grad_low, first_moment, second_moment):
    new_first = beta_first * first_moment + (1.0 - beta_first) * grad_low
    new_second = beta_second * second_moment + (1.0 - beta_second) * grad_low * grad_low
    corrected_first = new_first / (1.0 - beta_first**STEP)
    corrected_second = new_second / (1.0 - beta_second**STEP)
    direction = (corrected_first / (jnp.sqrt(corrected_second) + adam_epsilon)).astype(jnp.bfloat16)
    return (new_first, new_second, direction)


CHUNKS = 8
EARLY = 6


def spread_kernel(terms_ref, spread_ref):
    total = terms_ref[0].astype(jnp.float32)
    for split in range(1, terms_ref.shape[0]):
        total += terms_ref[split].astype(jnp.float32)
    share = total.astype(jnp.bfloat16)

    @pl.loop(0, spread_ref.shape[0])
    def _(chip):
        spread_ref[chip] = share


def sum_and_spread(terms, copies):
    return pl.pallas_call(
        spread_kernel,
        in_specs=[pl.BlockSpec(memory_space=pltpu.VMEM)],
        out_specs=pl.BlockSpec(memory_space=pltpu.VMEM),
        out_shape=jax.ShapeDtypeStruct((copies,) + terms.shape[1:], jnp.bfloat16),
        compiler_params=pltpu.CompilerParams(vmem_limit_bytes=8 * 1024 * 1024),
    )(terms)


def half_dot(side, projected_ref, grad_t_ref, first_chip, chips, skipped=0):
    rows = projected_ref.shape[2]
    at = lambda chip: pl.ds(pl.multiple_of((2 * (chip - skipped) + side) * rows, rows), rows)
    members = range(first_chip, first_chip + chips)
    projected = jnp.concatenate([projected_ref[chip] for chip in members], axis=1)
    grad_t = jnp.concatenate([grad_t_ref[:, at(chip)] for chip in members], axis=1)
    return lax.dot_general(
        grad_t, projected, (((1,), (1,)), ((), ())), preferred_element_type=jnp.float32
    )


def own_kernel(core_ref, own_ref, grad_t_ref, held_ref, partial_ref, sems):
    tokens = grad_t_ref.shape[1] // CHUNKS
    chips = own_ref.shape[0] // CHUNKS
    reads = []
    for chunk in range(EARLY):
        part = pl.ds(chunk * tokens, tokens)
        reads.append(
            pltpu.make_async_copy(grad_t_ref.at[:, part], held_ref.at[:, part], sems.at[chunk])
        )
        reads[-1].start()
    total = jnp.zeros(partial_ref.shape, jnp.float32)
    for chunk in range(EARLY):
        reads[chunk].wait()
        total += half_dot(core_ref[0], own_ref, held_ref, chunk * chips, chips)
    partial_ref[...] = total


def own_half(core, own, grad_t):
    chips, rank, rows = own.shape
    hidden, tokens = grad_t.shape
    return pl.pallas_call(
        own_kernel,
        in_specs=[
            pl.BlockSpec(memory_space=pltpu.SMEM),
            pl.BlockSpec(memory_space=pltpu.VMEM),
            pl.BlockSpec(memory_space=pltpu.HBM),
        ],
        out_specs=[pl.BlockSpec(memory_space=pltpu.VMEM), pl.BlockSpec(memory_space=pltpu.VMEM)],
        out_shape=[
            jax.ShapeDtypeStruct((hidden, tokens * EARLY // CHUNKS), jnp.bfloat16),
            jax.ShapeDtypeStruct((hidden, rank), jnp.float32),
        ],
        scratch_shapes=[pltpu.SemaphoreType.DMA((EARLY,))],
        compiler_params=pltpu.CompilerParams(vmem_limit_bytes=24 * 1024 * 1024),
        cost_estimate=pl.CostEstimate(
            flops=rank * hidden * tokens, bytes_accessed=2 * hidden * tokens, transcendentals=0
        ),
    )(core, own, grad_t)


def moments_kernel(core_ref, own_ref, other_ref, held_ref, grad_t_ref, partial_ref, first_ref, second_ref,
                   new_first_ref, new_second_ref, spread_ref, late_ref, first_in, second_in, sems):
    chips = other_ref.shape[0] // CHUNKS
    tokens = grad_t_ref.shape[1] // CHUNKS
    reads = []
    for chunk in range(EARLY, CHUNKS):
        part = pl.ds((chunk - EARLY) * tokens, tokens)
        reads.append(
            pltpu.make_async_copy(
                grad_t_ref.at[:, pl.ds(chunk * tokens, tokens)], late_ref.at[:, part], sems.at[chunk - EARLY]
            )
        )
    reads.append(pltpu.make_async_copy(first_ref, first_in, sems.at[CHUNKS - EARLY]))
    reads.append(pltpu.make_async_copy(second_ref, second_in, sems.at[CHUNKS - EARLY + 1]))
    for read in reads:
        read.start()
    side = core_ref[0]
    total = partial_ref[...]
    for chunk in range(EARLY):
        total += half_dot(1 - side, other_ref, held_ref, chunk * chips, chips)
    for chunk in range(EARLY, CHUNKS):
        reads[chunk - EARLY].wait()
        total += half_dot(side, own_ref, late_ref, chunk * chips, chips, EARLY * chips)
        total += half_dot(1 - side, other_ref, late_ref, chunk * chips, chips, EARLY * chips)
    for read in reads[CHUNKS - EARLY :]:
        read.wait()
    new_first, new_second, direction = moments_step(total.T, first_in[...], second_in[...])
    new_first_ref[...] = new_first
    new_second_ref[...] = new_second
    for copy in range(spread_ref.shape[0]):
        spread_ref[copy] = direction


def rest_and_moments(core, own, other, held, grad_t, partial, first_moment, second_moment, copies):
    rank, hidden = first_moment.shape
    vmem = pl.BlockSpec(memory_space=pltpu.VMEM)
    hbm = pl.BlockSpec(memory_space=pltpu.HBM)
    return pl.pallas_call(
        moments_kernel,
        in_specs=[pl.BlockSpec(memory_space=pltpu.SMEM), vmem, vmem, vmem, hbm, vmem, hbm, hbm],
        out_specs=[vmem, vmem, vmem],
        out_shape=[
            jax.ShapeDtypeStruct((rank, hidden), jnp.float32),
            jax.ShapeDtypeStruct((rank, hidden), jnp.float32),
            jax.ShapeDtypeStruct((copies, rank, hidden), jnp.bfloat16),
        ],
        scratch_shapes=[
            pltpu.VMEM((hidden, grad_t.shape[1] * (CHUNKS - EARLY) // CHUNKS), jnp.bfloat16),
            pltpu.VMEM((rank, hidden), jnp.float32),
            pltpu.VMEM((rank, hidden), jnp.float32),
            pltpu.SemaphoreType.DMA((CHUNKS - EARLY + 2,)),
        ],
        compiler_params=pltpu.CompilerParams(vmem_limit_bytes=24 * 1024 * 1024),
    )(core, own, other, held, grad_t, partial, first_moment, second_moment)


PARTS = 4


def project_kernel(acts_ref, basis_ref, terms_ref, acts_in, basis_in, sems):
    depth = acts_ref.shape[1] // PARTS
    reads = []
    for part in range(PARTS):
        at = pl.ds(part * depth, depth)
        reads.append(
            (
                pltpu.make_async_copy(acts_ref.at[:, at], acts_in.at[:, at], sems.at[0, part]),
                pltpu.make_async_copy(basis_ref.at[at, :], basis_in.at[at, :], sems.at[1, part]),
            )
        )
        for read in reads[-1]:
            read.start()
    total = jnp.zeros((acts_ref.shape[0], basis_ref.shape[1]), jnp.float32)
    for part in range(PARTS):
        for read in reads[part]:
            read.wait()
        at = pl.ds(part * depth, depth)
        total += jnp.dot(acts_in[:, at], basis_in[at, :], preferred_element_type=jnp.float32)
    terms_ref[...] = total.T.astype(jnp.bfloat16)


def project(acts, basis):
    tokens, ranks = acts.shape[0], basis.shape[1]
    hbm = pl.BlockSpec(memory_space=pltpu.HBM)
    return pl.pallas_call(
        project_kernel,
        in_specs=[hbm, hbm],
        out_specs=pl.BlockSpec(memory_space=pltpu.VMEM),
        out_shape=jax.ShapeDtypeStruct((ranks, tokens), jnp.bfloat16),
        scratch_shapes=[
            pltpu.VMEM(acts.shape, jnp.bfloat16),
            pltpu.VMEM(basis.shape, jnp.bfloat16),
            pltpu.SemaphoreType.DMA((2, PARTS)),
        ],
        compiler_params=pltpu.CompilerParams(vmem_limit_bytes=16 * 1024 * 1024),
    )(acts, basis)


def per_device(acts, out_grad, basis, first_moment, second_moment):
    splits = lax.axis_size("x")
    chips = lax.axis_size("z") * lax.axis_size("y")
    tokens = acts.shape[0]
    rank = basis.shape[1] // splits
    in_hbm = lambda array: pltpu.with_memory_space_constraint(array, pltpu.HBM)
    grad_t = in_hbm(out_grad.T)
    local_terms = project(in_hbm(acts), in_hbm(basis))
    terms = lax.all_to_all(
        local_terms.reshape(splits, rank, tokens), "x", split_axis=0, concat_axis=0, tiled=True
    )
    spread = sum_and_spread(terms, chips)
    own = lax.all_to_all(spread, ("z", "y"), split_axis=0, concat_axis=0, tiled=True)
    other = lax.ppermute(own, "c", [(0, 1), (1, 0)])
    core = lax.axis_index("c").astype(jnp.int32).reshape(1)
    held, partial = own_half(core, own, grad_t)
    new_first, new_second, direction = rest_and_moments(
        core, own, other, held, grad_t, partial, first_moment, second_moment, splits
    )
    pieces = lax.all_to_all(direction, "x", split_axis=0, concat_axis=0, tiled=True)
    piece = pieces.reshape(splits * rank, pieces.shape[2])
    update = jnp.dot(basis, piece, preferred_element_type=jnp.float32)
    return (update, new_first, new_second)


def solution(mesh):
    chips = Mesh(np.asarray(mesh.devices).reshape(8, 8, 8, 2), ("x", "z", "y", "c"))
    fsdp = ("z", "y", "c")
    return jax.shard_map(
        per_device,
        mesh=chips,
        in_specs=(P(fsdp, "x"), P(None, fsdp), P("x", None), P("x", fsdp), P("x", fsdp)),
        out_specs=(P("x", fsdp), P("x", fsdp), P("x", fsdp)),
        check_vma=False,
    )
```

```python
import jax
import jax.numpy as jnp
from jax import lax
from jax.experimental import pallas as pl
from jax.experimental.pallas import tpu as pltpu
from jax.sharding import PartitionSpec as P

STEP = 1000


beta_first = 0.9
beta_second = 0.999
adam_epsilon = 1e-08


def moments_step(grad_low, first_moment, second_moment):
    new_first = beta_first * first_moment + (1.0 - beta_first) * grad_low
    new_second = beta_second * second_moment + (1.0 - beta_second) * grad_low * grad_low
    corrected_first = new_first / (1.0 - beta_first**STEP)
    corrected_second = new_second / (1.0 - beta_second**STEP)
    direction = (corrected_first / (jnp.sqrt(corrected_second) + adam_epsilon)).astype(jnp.bfloat16)
    return (new_first, new_second, direction)


CHUNKS = 8
SIDE = 8
CORES = 2


def spread_kernel(terms_ref, spread_ref):
    total = terms_ref[0].astype(jnp.float32)
    for split in range(1, terms_ref.shape[0]):
        total += terms_ref[split].astype(jnp.float32)
    share = total.astype(jnp.bfloat16)

    @pl.loop(0, spread_ref.shape[0])
    def _(chip):
        spread_ref[chip] = share


def sum_and_spread(terms, copies):
    return pl.pallas_call(
        spread_kernel,
        in_specs=[pl.BlockSpec(memory_space=pltpu.VMEM)],
        out_specs=pl.BlockSpec(memory_space=pltpu.VMEM),
        out_shape=jax.ShapeDtypeStruct((copies,) + terms.shape[1:], jnp.bfloat16),
        compiler_params=pltpu.CompilerParams(vmem_limit_bytes=8 * 1024 * 1024),
    )(terms)


def half_dot(side, projected_ref, grad_t_ref, first_chip, chips):
    rows = projected_ref.shape[2]
    at = lambda chip: pl.ds(pl.multiple_of((2 * chip + side) * rows, rows), rows)
    members = range(first_chip, first_chip + chips)
    place = lambda chip: jnp.where(side == 0, chip, chip % SIDE * SIDE + chip // SIDE)
    projected = jnp.concatenate([projected_ref[place(chip)] for chip in members], axis=1)
    grad_t = jnp.concatenate([grad_t_ref[:, at(chip)] for chip in members], axis=1)
    return lax.dot_general(
        grad_t, projected, (((1,), (1,)), ((), ())), preferred_element_type=jnp.float32
    )


def own_kernel(core_ref, own_ref, grad_t_ref, held_ref, partial_ref, sems):
    tokens = grad_t_ref.shape[1] // CHUNKS
    chips = own_ref.shape[0] // CHUNKS
    copies = []
    for chunk in range(CHUNKS):
        part = pl.ds(chunk * tokens, tokens)
        copies.append(
            pltpu.make_async_copy(grad_t_ref.at[:, part], held_ref.at[:, part], sems.at[chunk])
        )
        copies[-1].start()
    total = jnp.zeros(partial_ref.shape, jnp.float32)
    for chunk in range(CHUNKS):
        copies[chunk].wait()
        total += half_dot(core_ref[0], own_ref, held_ref, chunk * chips, chips)
    partial_ref[...] = total


def own_half(core, own, grad_t):
    chips, rank, rows = own.shape
    hidden, tokens = grad_t.shape
    return pl.pallas_call(
        own_kernel,
        in_specs=[
            pl.BlockSpec(memory_space=pltpu.SMEM),
            pl.BlockSpec(memory_space=pltpu.VMEM),
            pl.BlockSpec(memory_space=pltpu.HBM),
        ],
        out_specs=[pl.BlockSpec(memory_space=pltpu.VMEM), pl.BlockSpec(memory_space=pltpu.VMEM)],
        out_shape=[
            jax.ShapeDtypeStruct((hidden, tokens), jnp.bfloat16),
            jax.ShapeDtypeStruct((hidden, rank), jnp.float32),
        ],
        scratch_shapes=[pltpu.SemaphoreType.DMA((CHUNKS,))],
        compiler_params=pltpu.CompilerParams(vmem_limit_bytes=24 * 1024 * 1024),
        cost_estimate=pl.CostEstimate(
            flops=2 * rank * hidden * tokens, bytes_accessed=4 * hidden * tokens, transcendentals=0
        ),
    )(core, own, grad_t)


def moments_kernel(core_ref, other_ref, held_ref, partial_ref, first_ref, second_ref,
                   new_first_ref, new_second_ref, spread_ref, first_in, second_in, sems):
    reads = [
        pltpu.make_async_copy(first_ref, first_in, sems.at[0]),
        pltpu.make_async_copy(second_ref, second_in, sems.at[1]),
    ]
    for read in reads:
        read.start()
    chips = other_ref.shape[0] // CHUNKS
    total = partial_ref[...]
    for chunk in range(CHUNKS):
        total += half_dot(1 - core_ref[0], other_ref, held_ref, chunk * chips, chips)
    for read in reads:
        read.wait()
    new_first, new_second, direction = moments_step(total.T, first_in[...], second_in[...])
    new_first_ref[...] = new_first
    new_second_ref[...] = new_second
    for copy in range(spread_ref.shape[0]):
        spread_ref[copy] = direction


def other_half_and_moments(core, other, held, partial, first_moment, second_moment, copies):
    rank, hidden = first_moment.shape
    vmem = pl.BlockSpec(memory_space=pltpu.VMEM)
    hbm = pl.BlockSpec(memory_space=pltpu.HBM)
    return pl.pallas_call(
        moments_kernel,
        in_specs=[pl.BlockSpec(memory_space=pltpu.SMEM), vmem, vmem, vmem, hbm, hbm],
        out_specs=[vmem, vmem, vmem],
        out_shape=[
            jax.ShapeDtypeStruct((rank, hidden), jnp.float32),
            jax.ShapeDtypeStruct((rank, hidden), jnp.float32),
            jax.ShapeDtypeStruct((copies, rank, hidden), jnp.bfloat16),
        ],
        scratch_shapes=[
            pltpu.VMEM((rank, hidden), jnp.float32),
            pltpu.VMEM((rank, hidden), jnp.float32),
            pltpu.SemaphoreType.DMA((2,)),
        ],
        compiler_params=pltpu.CompilerParams(vmem_limit_bytes=24 * 1024 * 1024),
    )(core, other, held, partial, first_moment, second_moment)


PARTS = 4


def project_kernel(acts_ref, basis_ref, terms_ref, acts_in, basis_in, sems):
    depth = acts_ref.shape[1] // PARTS
    reads = []
    for part in range(PARTS):
        at = pl.ds(part * depth, depth)
        reads.append(
            (
                pltpu.make_async_copy(acts_ref.at[:, at], acts_in.at[:, at], sems.at[0, part]),
                pltpu.make_async_copy(basis_ref.at[at, :], basis_in.at[at, :], sems.at[1, part]),
            )
        )
        for read in reads[-1]:
            read.start()
    total = jnp.zeros((acts_ref.shape[0], basis_ref.shape[1]), jnp.float32)
    for part in range(PARTS):
        for read in reads[part]:
            read.wait()
        at = pl.ds(part * depth, depth)
        total += jnp.dot(acts_in[:, at], basis_in[at, :], preferred_element_type=jnp.float32)
    terms_ref[...] = total.T.astype(jnp.bfloat16)


def project(acts, basis):
    tokens, ranks = acts.shape[0], basis.shape[1]
    hbm = pl.BlockSpec(memory_space=pltpu.HBM)
    return pl.pallas_call(
        project_kernel,
        in_specs=[hbm, hbm],
        out_specs=pl.BlockSpec(memory_space=pltpu.VMEM),
        out_shape=jax.ShapeDtypeStruct((ranks, tokens), jnp.bfloat16),
        scratch_shapes=[
            pltpu.VMEM(acts.shape, jnp.bfloat16),
            pltpu.VMEM(basis.shape, jnp.bfloat16),
            pltpu.SemaphoreType.DMA((2, PARTS)),
        ],
        compiler_params=pltpu.CompilerParams(vmem_limit_bytes=16 * 1024 * 1024),
    )(acts, basis)


def crossing(first):
    groups = []
    for at in range(SIDE):
        groups.append([(z * SIDE + at) * CORES + first for z in range(SIDE)])
        groups.append([(at * SIDE + y) * CORES + 1 - first for y in range(SIDE)])
    return groups


def exchange(block, first):
    copies = jnp.broadcast_to(block[None], (SIDE,) + block.shape)
    return lax.all_to_all(
        copies, "fsdp", split_axis=0, concat_axis=0, tiled=True, axis_index_groups=crossing(first)
    )


def per_device(acts, out_grad, basis, first_moment, second_moment):
    splits = lax.axis_size("dp")
    tokens = acts.shape[0]
    rank = basis.shape[1] // splits
    in_hbm = lambda array: pltpu.with_memory_space_constraint(array, pltpu.HBM)
    grad_t = in_hbm(out_grad.T)
    local_terms = project(in_hbm(acts), in_hbm(basis))
    terms = lax.all_to_all(
        local_terms.reshape(splits, rank, tokens), "dp", split_axis=0, concat_axis=0, tiled=True
    )
    line = lax.all_to_all(
        sum_and_spread(terms, SIDE), "fsdp", split_axis=0, concat_axis=0, tiled=True,
        axis_index_groups=crossing(1),
    )
    own = exchange(line, 0).reshape(SIDE * SIDE, rank, tokens)
    other = lax.ppermute(own, "fsdp", [(at, at ^ 1) for at in range(SIDE * SIDE * CORES)])
    core = (lax.axis_index("fsdp") & (CORES - 1)).astype(jnp.int32).reshape(1)
    held, partial = own_half(core, own, grad_t)
    new_first, new_second, direction = other_half_and_moments(
        core, other, held, partial, first_moment, second_moment, splits
    )
    pieces = lax.all_to_all(direction, "dp", split_axis=0, concat_axis=0, tiled=True)
    piece = pieces.reshape(splits * rank, pieces.shape[2])
    update = jnp.dot(basis, piece, preferred_element_type=jnp.float32)
    return (update, new_first, new_second)


def solution(mesh):
    return jax.shard_map(
        per_device,
        mesh=mesh,
        in_specs=(
            P("fsdp", "dp"),
            P(None, "fsdp"),
            P("dp", None),
            P("dp", "fsdp"),
            P("dp", "fsdp"),
        ),
        out_specs=(P("dp", "fsdp"), P("dp", "fsdp"), P("dp", "fsdp")),
        check_vma=False,
    )
```

```python
import jax
import jax.numpy as jnp
import numpy as np
from jax import lax
from jax.experimental import pallas as pl
from jax.experimental.pallas import tpu as pltpu
from jax.sharding import Mesh
from jax.sharding import PartitionSpec as P

STEP = 1000


beta_first = 0.9
beta_second = 0.999
adam_epsilon = 1e-08


def moments_step(grad_low, first_moment, second_moment):
    new_first = beta_first * first_moment + (1.0 - beta_first) * grad_low
    new_second = beta_second * second_moment + (1.0 - beta_second) * grad_low * grad_low
    corrected_first = new_first / (1.0 - beta_first**STEP)
    corrected_second = new_second / (1.0 - beta_second**STEP)
    direction = (corrected_first / (jnp.sqrt(corrected_second) + adam_epsilon)).astype(jnp.bfloat16)
    return (new_first, new_second, direction)


CHUNKS = 8


def spread_kernel(terms_ref, spread_ref):
    total = terms_ref[0].astype(jnp.float32)
    for split in range(1, terms_ref.shape[0]):
        total += terms_ref[split].astype(jnp.float32)
    share = total.astype(jnp.bfloat16)

    @pl.loop(0, spread_ref.shape[0])
    def _(chip):
        spread_ref[chip] = share


def sum_and_spread(terms, copies):
    return pl.pallas_call(
        spread_kernel,
        in_specs=[pl.BlockSpec(memory_space=pltpu.VMEM)],
        out_specs=pl.BlockSpec(memory_space=pltpu.VMEM),
        out_shape=jax.ShapeDtypeStruct((copies,) + terms.shape[1:], jnp.bfloat16),
        compiler_params=pltpu.CompilerParams(vmem_limit_bytes=8 * 1024 * 1024),
    )(terms)


def half_dot(side, projected_ref, grad_t_ref, first_chip, chips):
    rows = projected_ref.shape[2]
    at = lambda chip: pl.ds(pl.multiple_of((2 * chip + side) * rows, rows), rows)
    members = range(first_chip, first_chip + chips)
    projected = jnp.concatenate([projected_ref[chip] for chip in members], axis=1)
    grad_t = jnp.concatenate([grad_t_ref[:, at(chip)] for chip in members], axis=1)
    return lax.dot_general(
        grad_t, projected, (((1,), (1,)), ((), ())), preferred_element_type=jnp.float32
    )


def own_kernel(core_ref, own_ref, grad_t_ref, held_ref, partial_ref, sems):
    tokens = grad_t_ref.shape[1] // CHUNKS
    chips = own_ref.shape[0] // CHUNKS
    copies = []
    for chunk in range(CHUNKS):
        part = pl.ds(chunk * tokens, tokens)
        copies.append(
            pltpu.make_async_copy(grad_t_ref.at[:, part], held_ref.at[:, part], sems.at[chunk])
        )
        copies[-1].start()
    total = jnp.zeros(partial_ref.shape, jnp.float32)
    for chunk in range(CHUNKS):
        copies[chunk].wait()
        total += half_dot(core_ref[0], own_ref, held_ref, chunk * chips, chips)
    partial_ref[...] = total


def own_half(core, own, grad_t):
    chips, rank, rows = own.shape
    hidden, tokens = grad_t.shape
    return pl.pallas_call(
        own_kernel,
        in_specs=[
            pl.BlockSpec(memory_space=pltpu.SMEM),
            pl.BlockSpec(memory_space=pltpu.VMEM),
            pl.BlockSpec(memory_space=pltpu.HBM),
        ],
        out_specs=[pl.BlockSpec(memory_space=pltpu.VMEM), pl.BlockSpec(memory_space=pltpu.VMEM)],
        out_shape=[
            jax.ShapeDtypeStruct((hidden, tokens), jnp.bfloat16),
            jax.ShapeDtypeStruct((hidden, rank), jnp.float32),
        ],
        scratch_shapes=[pltpu.SemaphoreType.DMA((CHUNKS,))],
        compiler_params=pltpu.CompilerParams(vmem_limit_bytes=24 * 1024 * 1024),
        cost_estimate=pl.CostEstimate(
            flops=2 * rank * hidden * tokens, bytes_accessed=4 * hidden * tokens, transcendentals=0
        ),
    )(core, own, grad_t)


def moments_kernel(core_ref, other_ref, held_ref, partial_ref, first_ref, second_ref,
                   new_first_ref, new_second_ref, spread_ref, first_in, second_in, sems):
    reads = [
        pltpu.make_async_copy(first_ref, first_in, sems.at[0]),
        pltpu.make_async_copy(second_ref, second_in, sems.at[1]),
    ]
    for read in reads:
        read.start()
    chips = other_ref.shape[0] // CHUNKS
    total = partial_ref[...]
    for chunk in range(CHUNKS):
        total += half_dot(1 - core_ref[0], other_ref, held_ref, chunk * chips, chips)
    for read in reads:
        read.wait()
    new_first, new_second, direction = moments_step(total.T, first_in[...], second_in[...])
    new_first_ref[...] = new_first
    new_second_ref[...] = new_second
    for copy in range(spread_ref.shape[0]):
        spread_ref[copy] = direction


def other_half_and_moments(core, other, held, partial, first_moment, second_moment, copies):
    rank, hidden = first_moment.shape
    vmem = pl.BlockSpec(memory_space=pltpu.VMEM)
    hbm = pl.BlockSpec(memory_space=pltpu.HBM)
    return pl.pallas_call(
        moments_kernel,
        in_specs=[pl.BlockSpec(memory_space=pltpu.SMEM), vmem, vmem, vmem, hbm, hbm],
        out_specs=[vmem, vmem, vmem],
        out_shape=[
            jax.ShapeDtypeStruct((rank, hidden), jnp.float32),
            jax.ShapeDtypeStruct((rank, hidden), jnp.float32),
            jax.ShapeDtypeStruct((copies, rank, hidden), jnp.bfloat16),
        ],
        scratch_shapes=[
            pltpu.VMEM((rank, hidden), jnp.float32),
            pltpu.VMEM((rank, hidden), jnp.float32),
            pltpu.SemaphoreType.DMA((2,)),
        ],
        compiler_params=pltpu.CompilerParams(vmem_limit_bytes=24 * 1024 * 1024),
    )(core, other, held, partial, first_moment, second_moment)


PARTS = 4


def project_kernel(acts_ref, basis_ref, terms_ref, acts_in, basis_in, sems):
    depth = acts_ref.shape[1] // PARTS
    reads = []
    for part in range(PARTS):
        at = pl.ds(part * depth, depth)
        reads.append(
            (
                pltpu.make_async_copy(acts_ref.at[:, at], acts_in.at[:, at], sems.at[0, part]),
                pltpu.make_async_copy(basis_ref.at[at, :], basis_in.at[at, :], sems.at[1, part]),
            )
        )
        for read in reads[-1]:
            read.start()
    total = jnp.zeros((acts_ref.shape[0], basis_ref.shape[1]), jnp.float32)
    for part in range(PARTS):
        for read in reads[part]:
            read.wait()
        at = pl.ds(part * depth, depth)
        total += jnp.dot(acts_in[:, at], basis_in[at, :], preferred_element_type=jnp.float32)
    terms_ref[...] = total.T.astype(jnp.bfloat16)


def project(acts, basis):
    tokens, ranks = acts.shape[0], basis.shape[1]
    hbm = pl.BlockSpec(memory_space=pltpu.HBM)
    return pl.pallas_call(
        project_kernel,
        in_specs=[hbm, hbm],
        out_specs=pl.BlockSpec(memory_space=pltpu.VMEM),
        out_shape=jax.ShapeDtypeStruct((ranks, tokens), jnp.bfloat16),
        scratch_shapes=[
            pltpu.VMEM(acts.shape, jnp.bfloat16),
            pltpu.VMEM(basis.shape, jnp.bfloat16),
            pltpu.SemaphoreType.DMA((2, PARTS)),
        ],
        compiler_params=pltpu.CompilerParams(vmem_limit_bytes=16 * 1024 * 1024),
    )(acts, basis)


def per_device(acts, out_grad, basis, first_moment, second_moment):
    splits = lax.axis_size("x")
    chips = lax.axis_size("z") * lax.axis_size("y")
    tokens = acts.shape[0]
    rank = basis.shape[1] // splits
    in_hbm = lambda array: pltpu.with_memory_space_constraint(array, pltpu.HBM)
    grad_t = in_hbm(out_grad.T)
    local_terms = project(in_hbm(acts), in_hbm(basis))
    terms = lax.all_to_all(
        local_terms.reshape(splits, rank, tokens), "x", split_axis=0, concat_axis=0, tiled=True
    )
    spread = sum_and_spread(terms, chips)
    own = lax.all_to_all(spread, ("z", "y"), split_axis=0, concat_axis=0, tiled=True)
    other = lax.ppermute(own, "c", [(0, 1), (1, 0)])
    core = lax.axis_index("c").astype(jnp.int32).reshape(1)
    held, partial = own_half(core, own, grad_t)
    new_first, new_second, direction = other_half_and_moments(
        core, other, held, partial, first_moment, second_moment, splits
    )
    pieces = lax.all_to_all(direction, "x", split_axis=0, concat_axis=0, tiled=True)
    piece = pieces.reshape(splits * rank, pieces.shape[2])
    update = jnp.dot(basis, piece, preferred_element_type=jnp.float32)
    return (update, new_first, new_second)


def solution(mesh):
    chips = Mesh(np.asarray(mesh.devices).reshape(8, 8, 8, 2), ("x", "z", "y", "c"))
    fsdp = ("z", "y", "c")
    return jax.shard_map(
        per_device,
        mesh=chips,
        in_specs=(P(fsdp, "x"), P(None, fsdp), P("x", None), P("x", fsdp), P("x", fsdp)),
        out_specs=(P("x", fsdp), P("x", fsdp), P("x", fsdp)),
        check_vma=False,
    )
```

```python
import jax
import jax.numpy as jnp
from jax import lax
from jax.experimental import pallas as pl
from jax.experimental.pallas import tpu as pltpu
from jax.sharding import PartitionSpec as P

STEP = 1000


beta_first = 0.9
beta_second = 0.999
adam_epsilon = 1e-08


def moments_step(grad_low, first_moment, second_moment):
    new_first = beta_first * first_moment + (1.0 - beta_first) * grad_low
    new_second = beta_second * second_moment + (1.0 - beta_second) * grad_low * grad_low
    corrected_first = new_first / (1.0 - beta_first**STEP)
    corrected_second = new_second / (1.0 - beta_second**STEP)
    direction = (corrected_first / (jnp.sqrt(corrected_second) + adam_epsilon)).astype(jnp.bfloat16)
    return (new_first, new_second, direction)


CHUNKS = 8
SIDE = 8
CORES = 2


def spread_kernel(terms_ref, spread_ref):
    total = terms_ref[0].astype(jnp.float32)
    for split in range(1, terms_ref.shape[0]):
        total += terms_ref[split].astype(jnp.float32)
    share = total.astype(jnp.bfloat16)

    @pl.loop(0, spread_ref.shape[0])
    def _(chip):
        spread_ref[chip] = share


def sum_and_spread(terms, copies):
    return pl.pallas_call(
        spread_kernel,
        in_specs=[pl.BlockSpec(memory_space=pltpu.VMEM)],
        out_specs=pl.BlockSpec(memory_space=pltpu.VMEM),
        out_shape=jax.ShapeDtypeStruct((copies,) + terms.shape[1:], jnp.bfloat16),
        compiler_params=pltpu.CompilerParams(vmem_limit_bytes=8 * 1024 * 1024),
    )(terms)


def half_dot(side, projected_ref, grad_t_ref, first_chip, chips):
    rows = projected_ref.shape[2]
    at = lambda chip: pl.ds(pl.multiple_of((2 * chip + side) * rows, rows), rows)
    members = range(first_chip, first_chip + chips)
    place = lambda chip: jnp.where(side == 1, chip, chip % SIDE * SIDE + chip // SIDE)
    projected = jnp.concatenate([projected_ref[place(chip)] for chip in members], axis=1)
    grad_t = jnp.concatenate([grad_t_ref[:, at(chip)] for chip in members], axis=1)
    return lax.dot_general(
        grad_t, projected, (((1,), (1,)), ((), ())), preferred_element_type=jnp.float32
    )


def own_kernel(core_ref, own_ref, grad_t_ref, held_ref, partial_ref, sems):
    tokens = grad_t_ref.shape[1] // CHUNKS
    chips = own_ref.shape[0] // CHUNKS
    copies = []
    for chunk in range(CHUNKS):
        part = pl.ds(chunk * tokens, tokens)
        copies.append(
            pltpu.make_async_copy(grad_t_ref.at[:, part], held_ref.at[:, part], sems.at[chunk])
        )
        copies[-1].start()
    total = jnp.zeros(partial_ref.shape, jnp.float32)
    for chunk in range(CHUNKS):
        copies[chunk].wait()
        total += half_dot(core_ref[0], own_ref, held_ref, chunk * chips, chips)
    partial_ref[...] = total


def own_half(core, own, grad_t):
    chips, rank, rows = own.shape
    hidden, tokens = grad_t.shape
    return pl.pallas_call(
        own_kernel,
        in_specs=[
            pl.BlockSpec(memory_space=pltpu.SMEM),
            pl.BlockSpec(memory_space=pltpu.VMEM),
            pl.BlockSpec(memory_space=pltpu.HBM),
        ],
        out_specs=[pl.BlockSpec(memory_space=pltpu.VMEM), pl.BlockSpec(memory_space=pltpu.VMEM)],
        out_shape=[
            jax.ShapeDtypeStruct((hidden, tokens), jnp.bfloat16),
            jax.ShapeDtypeStruct((hidden, rank), jnp.float32),
        ],
        scratch_shapes=[pltpu.SemaphoreType.DMA((CHUNKS,))],
        compiler_params=pltpu.CompilerParams(vmem_limit_bytes=24 * 1024 * 1024),
        cost_estimate=pl.CostEstimate(
            flops=2 * rank * hidden * tokens, bytes_accessed=4 * hidden * tokens, transcendentals=0
        ),
    )(core, own, grad_t)


def moments_kernel(core_ref, other_ref, held_ref, partial_ref, first_ref, second_ref,
                   new_first_ref, new_second_ref, spread_ref, first_in, second_in, sems):
    reads = [
        pltpu.make_async_copy(first_ref, first_in, sems.at[0]),
        pltpu.make_async_copy(second_ref, second_in, sems.at[1]),
    ]
    for read in reads:
        read.start()
    chips = other_ref.shape[0] // CHUNKS
    total = partial_ref[...]
    for chunk in range(CHUNKS):
        total += half_dot(1 - core_ref[0], other_ref, held_ref, chunk * chips, chips)
    for read in reads:
        read.wait()
    new_first, new_second, direction = moments_step(total.T, first_in[...], second_in[...])
    new_first_ref[...] = new_first
    new_second_ref[...] = new_second
    for copy in range(spread_ref.shape[0]):
        spread_ref[copy] = direction


def other_half_and_moments(core, other, held, partial, first_moment, second_moment, copies):
    rank, hidden = first_moment.shape
    vmem = pl.BlockSpec(memory_space=pltpu.VMEM)
    hbm = pl.BlockSpec(memory_space=pltpu.HBM)
    return pl.pallas_call(
        moments_kernel,
        in_specs=[pl.BlockSpec(memory_space=pltpu.SMEM), vmem, vmem, vmem, hbm, hbm],
        out_specs=[vmem, vmem, vmem],
        out_shape=[
            jax.ShapeDtypeStruct((rank, hidden), jnp.float32),
            jax.ShapeDtypeStruct((rank, hidden), jnp.float32),
            jax.ShapeDtypeStruct((copies, rank, hidden), jnp.bfloat16),
        ],
        scratch_shapes=[
            pltpu.VMEM((rank, hidden), jnp.float32),
            pltpu.VMEM((rank, hidden), jnp.float32),
            pltpu.SemaphoreType.DMA((2,)),
        ],
        compiler_params=pltpu.CompilerParams(vmem_limit_bytes=24 * 1024 * 1024),
    )(core, other, held, partial, first_moment, second_moment)


PARTS = 4


def project_kernel(acts_ref, basis_ref, terms_ref, acts_in, basis_in, sems):
    depth = acts_ref.shape[1] // PARTS
    reads = []
    for part in range(PARTS):
        at = pl.ds(part * depth, depth)
        reads.append(
            (
                pltpu.make_async_copy(acts_ref.at[:, at], acts_in.at[:, at], sems.at[0, part]),
                pltpu.make_async_copy(basis_ref.at[at, :], basis_in.at[at, :], sems.at[1, part]),
            )
        )
        for read in reads[-1]:
            read.start()
    total = jnp.zeros((acts_ref.shape[0], basis_ref.shape[1]), jnp.float32)
    for part in range(PARTS):
        for read in reads[part]:
            read.wait()
        at = pl.ds(part * depth, depth)
        total += jnp.dot(acts_in[:, at], basis_in[at, :], preferred_element_type=jnp.float32)
    terms_ref[...] = total.T.astype(jnp.bfloat16)


def project(acts, basis):
    tokens, ranks = acts.shape[0], basis.shape[1]
    hbm = pl.BlockSpec(memory_space=pltpu.HBM)
    return pl.pallas_call(
        project_kernel,
        in_specs=[hbm, hbm],
        out_specs=pl.BlockSpec(memory_space=pltpu.VMEM),
        out_shape=jax.ShapeDtypeStruct((ranks, tokens), jnp.bfloat16),
        scratch_shapes=[
            pltpu.VMEM(acts.shape, jnp.bfloat16),
            pltpu.VMEM(basis.shape, jnp.bfloat16),
            pltpu.SemaphoreType.DMA((2, PARTS)),
        ],
        compiler_params=pltpu.CompilerParams(vmem_limit_bytes=16 * 1024 * 1024),
    )(acts, basis)


def crossing(first):
    groups = []
    for at in range(SIDE):
        groups.append([(z * SIDE + at) * CORES + first for z in range(SIDE)])
        groups.append([(at * SIDE + y) * CORES + 1 - first for y in range(SIDE)])
    return groups


def exchange(block, first):
    copies = jnp.broadcast_to(block[None], (SIDE,) + block.shape)
    return lax.all_to_all(
        copies, "fsdp", split_axis=0, concat_axis=0, tiled=True, axis_index_groups=crossing(first)
    )


def per_device(acts, out_grad, basis, first_moment, second_moment):
    splits = lax.axis_size("dp")
    tokens = acts.shape[0]
    rank = basis.shape[1] // splits
    in_hbm = lambda array: pltpu.with_memory_space_constraint(array, pltpu.HBM)
    grad_t = in_hbm(out_grad.T)
    local_terms = project(in_hbm(acts), in_hbm(basis))
    terms = lax.all_to_all(
        local_terms.reshape(splits, rank, tokens), "dp", split_axis=0, concat_axis=0, tiled=True
    )
    line = lax.all_to_all(
        sum_and_spread(terms, SIDE), "fsdp", split_axis=0, concat_axis=0, tiled=True,
        axis_index_groups=crossing(0),
    )
    own = exchange(line, 1).reshape(SIDE * SIDE, rank, tokens)
    other = lax.ppermute(own, "fsdp", [(at, at ^ 1) for at in range(SIDE * SIDE * CORES)])
    core = (lax.axis_index("fsdp") & (CORES - 1)).astype(jnp.int32).reshape(1)
    held, partial = own_half(core, own, grad_t)
    new_first, new_second, direction = other_half_and_moments(
        core, other, held, partial, first_moment, second_moment, splits
    )
    pieces = lax.all_to_all(direction, "dp", split_axis=0, concat_axis=0, tiled=True)
    piece = pieces.reshape(splits * rank, pieces.shape[2])
    update = jnp.dot(basis, piece, preferred_element_type=jnp.float32)
    return (update, new_first, new_second)


def solution(mesh):
    return jax.shard_map(
        per_device,
        mesh=mesh,
        in_specs=(
            P("fsdp", "dp"),
            P(None, "fsdp"),
            P("dp", None),
            P("dp", "fsdp"),
            P("dp", "fsdp"),
        ),
        out_specs=(P("dp", "fsdp"), P("dp", "fsdp"), P("dp", "fsdp")),
        check_vma=False,
    )
```

```python
import jax
import jax.numpy as jnp
import numpy as np
from jax import lax
from jax.experimental import pallas as pl
from jax.experimental.pallas import tpu as pltpu
from jax.sharding import Mesh
from jax.sharding import PartitionSpec as P

STEP = 1000


beta_first = 0.9
beta_second = 0.999
adam_epsilon = 1e-08


def moments_step(grad_low, first_moment, second_moment):
    new_first = beta_first * first_moment + (1.0 - beta_first) * grad_low
    new_second = beta_second * second_moment + (1.0 - beta_second) * grad_low * grad_low
    corrected_first = new_first / (1.0 - beta_first**STEP)
    corrected_second = new_second / (1.0 - beta_second**STEP)
    direction = (corrected_first / (jnp.sqrt(corrected_second) + adam_epsilon)).astype(jnp.bfloat16)
    return (new_first, new_second, direction)


CHUNKS = 8
LANES = 128
STRIPS = 4


def pack(block):
    rows, tail = block.shape[0], block.shape[1] - LANES
    kept = rows * tail // LANES
    step = rows - kept
    last = [block[kept:, LANES + at : LANES + at + LANES - tail] for at in range(0, tail, LANES - tail)]
    assert len(last) * step == kept
    below = jnp.concatenate([block[:kept, LANES:], jnp.concatenate(last, axis=0)], axis=1)
    return jnp.concatenate([block[:, :LANES], below], axis=0)


def unpack(packed, rows, tail):
    kept = packed.shape[0] - rows
    step = rows - kept
    beside = packed[rows:, tail:]
    last = jnp.concatenate([beside[at : at + step] for at in range(0, kept, step)], axis=1)
    tails = jnp.concatenate([packed[rows:, :tail], last], axis=0)
    return jnp.concatenate([packed[:rows], tails], axis=1)


def spread_kernel(terms_ref, spread_ref):
    total = terms_ref[0].astype(jnp.float32)
    for split in range(1, terms_ref.shape[0]):
        total += terms_ref[split].astype(jnp.float32)
    share = total.astype(jnp.bfloat16)

    @pl.loop(0, spread_ref.shape[0])
    def _(chip):
        spread_ref[chip] = share


def sum_and_spread(terms, copies):
    return pl.pallas_call(
        spread_kernel,
        in_specs=[pl.BlockSpec(memory_space=pltpu.VMEM)],
        out_specs=pl.BlockSpec(memory_space=pltpu.VMEM),
        out_shape=jax.ShapeDtypeStruct((copies,) + terms.shape[1:], jnp.bfloat16),
        compiler_params=pltpu.CompilerParams(vmem_limit_bytes=8 * 1024 * 1024),
    )(terms)


def half_dot(side, projected_ref, grad_t_ref, first_chip, chips):
    rows = projected_ref.shape[2]
    at = lambda chip: pl.ds(pl.multiple_of((2 * chip + side) * rows, rows), rows)
    members = range(first_chip, first_chip + chips)
    projected = jnp.concatenate([projected_ref[chip] for chip in members], axis=1)
    grad_t = jnp.concatenate([grad_t_ref[:, at(chip)] for chip in members], axis=1)
    return lax.dot_general(
        grad_t, projected, (((1,), (1,)), ((), ())), preferred_element_type=jnp.float32
    )


def own_kernel(core_ref, own_ref, grad_t_ref, held_ref, partial_ref, sems):
    tokens = grad_t_ref.shape[1] // CHUNKS
    chips = own_ref.shape[0] // CHUNKS
    copies = []
    for chunk in range(CHUNKS):
        part = pl.ds(chunk * tokens, tokens)
        copies.append(
            pltpu.make_async_copy(grad_t_ref.at[:, part], held_ref.at[:, part], sems.at[chunk])
        )
        copies[-1].start()
    total = jnp.zeros(partial_ref.shape, jnp.float32)
    for chunk in range(CHUNKS):
        copies[chunk].wait()
        total += half_dot(core_ref[0], own_ref, held_ref, chunk * chips, chips)
    partial_ref[...] = total


def own_half(core, own, grad_t):
    chips, rank, rows = own.shape
    hidden, tokens = grad_t.shape
    return pl.pallas_call(
        own_kernel,
        in_specs=[
            pl.BlockSpec(memory_space=pltpu.SMEM),
            pl.BlockSpec(memory_space=pltpu.VMEM),
            pl.BlockSpec(memory_space=pltpu.HBM),
        ],
        out_specs=[pl.BlockSpec(memory_space=pltpu.VMEM), pl.BlockSpec(memory_space=pltpu.VMEM)],
        out_shape=[
            jax.ShapeDtypeStruct((hidden, tokens), jnp.bfloat16),
            jax.ShapeDtypeStruct((hidden, rank), jnp.float32),
        ],
        scratch_shapes=[pltpu.SemaphoreType.DMA((CHUNKS,))],
        compiler_params=pltpu.CompilerParams(vmem_limit_bytes=24 * 1024 * 1024),
        cost_estimate=pl.CostEstimate(
            flops=2 * rank * hidden * tokens, bytes_accessed=4 * hidden * tokens, transcendentals=0
        ),
    )(core, own, grad_t)


def moments_kernel(core_ref, other_ref, held_ref, partial_ref, first_ref, second_ref,
                   new_first_ref, new_second_ref, spread_ref, first_in, second_in, sems):
    reads = [
        pltpu.make_async_copy(first_ref, first_in, sems.at[0]),
        pltpu.make_async_copy(second_ref, second_in, sems.at[1]),
    ]
    for read in reads:
        read.start()
    chips = other_ref.shape[0] // CHUNKS
    total = partial_ref[...]
    for chunk in range(CHUNKS):
        total += half_dot(1 - core_ref[0], other_ref, held_ref, chunk * chips, chips)
    for read in reads:
        read.wait()
    new_first, new_second, direction = moments_step(total.T, first_in[...], second_in[...])
    new_first_ref[...] = new_first
    new_second_ref[...] = new_second
    packed = pack(direction)
    for copy in range(spread_ref.shape[0]):
        spread_ref[copy] = packed


def other_half_and_moments(core, other, held, partial, first_moment, second_moment, copies):
    rank, hidden = first_moment.shape
    vmem = pl.BlockSpec(memory_space=pltpu.VMEM)
    hbm = pl.BlockSpec(memory_space=pltpu.HBM)
    return pl.pallas_call(
        moments_kernel,
        in_specs=[pl.BlockSpec(memory_space=pltpu.SMEM), vmem, vmem, vmem, hbm, hbm],
        out_specs=[vmem, vmem, vmem],
        out_shape=[
            jax.ShapeDtypeStruct((rank, hidden), jnp.float32),
            jax.ShapeDtypeStruct((rank, hidden), jnp.float32),
            jax.ShapeDtypeStruct((copies, rank * hidden // LANES, LANES), jnp.bfloat16),
        ],
        scratch_shapes=[
            pltpu.VMEM((rank, hidden), jnp.float32),
            pltpu.VMEM((rank, hidden), jnp.float32),
            pltpu.SemaphoreType.DMA((2,)),
        ],
        compiler_params=pltpu.CompilerParams(vmem_limit_bytes=24 * 1024 * 1024),
    )(core, other, held, partial, first_moment, second_moment)


PARTS = 4


def project_kernel(acts_ref, basis_ref, terms_ref, acts_in, basis_in, sems):
    depth = acts_ref.shape[1] // PARTS
    reads = []
    for part in range(PARTS):
        at = pl.ds(part * depth, depth)
        reads.append(
            (
                pltpu.make_async_copy(acts_ref.at[:, at], acts_in.at[:, at], sems.at[0, part]),
                pltpu.make_async_copy(basis_ref.at[at, :], basis_in.at[at, :], sems.at[1, part]),
            )
        )
        for read in reads[-1]:
            read.start()
    total = jnp.zeros((acts_ref.shape[0], basis_ref.shape[1]), jnp.float32)
    for part in range(PARTS):
        for read in reads[part]:
            read.wait()
        at = pl.ds(part * depth, depth)
        total += jnp.dot(acts_in[:, at], basis_in[at, :], preferred_element_type=jnp.float32)
    terms_ref[...] = total.T.astype(jnp.bfloat16)


def project(acts, basis):
    tokens, ranks = acts.shape[0], basis.shape[1]
    hbm = pl.BlockSpec(memory_space=pltpu.HBM)
    return pl.pallas_call(
        project_kernel,
        in_specs=[hbm, hbm],
        out_specs=pl.BlockSpec(memory_space=pltpu.VMEM),
        out_shape=jax.ShapeDtypeStruct((ranks, tokens), jnp.bfloat16),
        scratch_shapes=[
            pltpu.VMEM(acts.shape, jnp.bfloat16),
            pltpu.VMEM(basis.shape, jnp.bfloat16),
            pltpu.SemaphoreType.DMA((2, PARTS)),
        ],
        compiler_params=pltpu.CompilerParams(vmem_limit_bytes=16 * 1024 * 1024),
    )(acts, basis)


def update_kernel(pieces_ref, basis_ref, update_t_ref, strips_ref, sems):
    hidden = update_t_ref.shape[0]
    rank = basis_ref.shape[1] // pieces_ref.shape[0]
    direction = jnp.concatenate(
        [unpack(pieces_ref[split], rank, hidden - LANES) for split in range(pieces_ref.shape[0])], axis=0
    )
    direction_t = direction.T
    width = basis_ref.shape[0] // STRIPS
    writes = []
    for strip in range(STRIPS):
        at = pl.ds(strip * width, width)
        strips_ref[:, at] = lax.dot_general(
            direction_t, basis_ref[at, :], (((1,), (1,)), ((), ())), preferred_element_type=jnp.float32
        )
        writes.append(
            pltpu.make_async_copy(strips_ref.at[:, at], update_t_ref.at[:, at], sems.at[strip])
        )
        writes[-1].start()
    for write in writes:
        write.wait()


def expand(pieces, basis, hidden):
    vmem = pl.BlockSpec(memory_space=pltpu.VMEM)
    return pl.pallas_call(
        update_kernel,
        in_specs=[vmem, vmem],
        out_specs=pl.BlockSpec(memory_space=pltpu.HBM),
        out_shape=jax.ShapeDtypeStruct((hidden, basis.shape[0]), jnp.float32),
        scratch_shapes=[
            pltpu.VMEM((hidden, basis.shape[0]), jnp.float32),
            pltpu.SemaphoreType.DMA((STRIPS,)),
        ],
        compiler_params=pltpu.CompilerParams(vmem_limit_bytes=24 * 1024 * 1024),
    )(pieces, basis)


def per_device(acts, out_grad, basis, first_moment, second_moment):
    splits = lax.axis_size("x")
    chips = lax.axis_size("z") * lax.axis_size("y")
    tokens = acts.shape[0]
    rank = basis.shape[1] // splits
    in_hbm = lambda array: pltpu.with_memory_space_constraint(array, pltpu.HBM)
    grad_t = in_hbm(out_grad.T)
    local_terms = project(in_hbm(acts), in_hbm(basis))
    terms = lax.all_to_all(
        local_terms.reshape(splits, rank, tokens), "x", split_axis=0, concat_axis=0, tiled=True
    )
    spread = sum_and_spread(terms, chips)
    own = lax.all_to_all(spread, ("z", "y"), split_axis=0, concat_axis=0, tiled=True)
    other = lax.ppermute(own, "c", [(0, 1), (1, 0)])
    core = lax.axis_index("c").astype(jnp.int32).reshape(1)
    held, partial = own_half(core, own, grad_t)
    new_first, new_second, direction = other_half_and_moments(
        core, other, held, partial, first_moment, second_moment, splits
    )
    pieces = lax.all_to_all(direction, "x", split_axis=0, concat_axis=0, tiled=True)
    update = expand(pieces, basis, first_moment.shape[1]).T
    return (update, new_first, new_second)


def solution(mesh):
    chips = Mesh(np.asarray(mesh.devices).reshape(8, 8, 8, 2), ("x", "z", "y", "c"))
    fsdp = ("z", "y", "c")
    return jax.shard_map(
        per_device,
        mesh=chips,
        in_specs=(P(fsdp, "x"), P(None, fsdp), P("x", None), P("x", fsdp), P("x", fsdp)),
        out_specs=(P("x", fsdp), P("x", fsdp), P("x", fsdp)),
        check_vma=False,
    )
```

```python
import jax
import jax.numpy as jnp
import numpy as np
from jax import lax
from jax.experimental import pallas as pl
from jax.experimental.pallas import tpu as pltpu
from jax.sharding import Mesh
from jax.sharding import PartitionSpec as P

STEP = 1000


beta_first = 0.9
beta_second = 0.999
adam_epsilon = 1e-08


def moments_step(grad_low, first_moment, second_moment):
    new_first = beta_first * first_moment + (1.0 - beta_first) * grad_low
    new_second = beta_second * second_moment + (1.0 - beta_second) * grad_low * grad_low
    corrected_first = new_first / (1.0 - beta_first**STEP)
    corrected_second = new_second / (1.0 - beta_second**STEP)
    direction = (corrected_first / (jnp.sqrt(corrected_second) + adam_epsilon)).astype(jnp.bfloat16)
    return (new_first, new_second, direction)


CHUNKS = 16
PIECES = 4
LANES = 128
STRIPS = 4


def pack(block):
    rows, tail = block.shape[0], block.shape[1] - LANES
    kept = rows * tail // LANES
    step = rows - kept
    last = [block[kept:, LANES + at : LANES + at + LANES - tail] for at in range(0, tail, LANES - tail)]
    assert len(last) * step == kept
    below = jnp.concatenate([block[:kept, LANES:], jnp.concatenate(last, axis=0)], axis=1)
    return jnp.concatenate([block[:, :LANES], below], axis=0)


def unpack(packed, rows, tail):
    kept = packed.shape[0] - rows
    step = rows - kept
    beside = packed[rows:, tail:]
    last = jnp.concatenate([beside[at : at + step] for at in range(0, kept, step)], axis=1)
    tails = jnp.concatenate([packed[rows:, :tail], last], axis=0)
    return jnp.concatenate([packed[:rows], tails], axis=1)


def spread_kernel(terms_ref, spread_ref):
    total = terms_ref[0].astype(jnp.float32)
    for split in range(1, terms_ref.shape[0]):
        total += terms_ref[split].astype(jnp.float32)
    share = total.astype(jnp.bfloat16)

    @pl.loop(0, spread_ref.shape[0])
    def _(chip):
        spread_ref[chip] = share


def sum_and_spread(terms, copies):
    return pl.pallas_call(
        spread_kernel,
        in_specs=[pl.BlockSpec(memory_space=pltpu.VMEM)],
        out_specs=pl.BlockSpec(memory_space=pltpu.VMEM),
        out_shape=jax.ShapeDtypeStruct((copies,) + terms.shape[1:], jnp.bfloat16),
        compiler_params=pltpu.CompilerParams(vmem_limit_bytes=8 * 1024 * 1024),
    )(terms)


def half_dot(side, projected_ref, grad_t_ref, first_chip, chips):
    rows = projected_ref.shape[2]
    at = lambda chip: pl.ds(pl.multiple_of((2 * chip + side) * rows, rows), rows)
    members = range(first_chip, first_chip + chips)
    projected = jnp.concatenate([projected_ref[chip] for chip in members], axis=1)
    grad_t = jnp.concatenate([grad_t_ref[:, at(chip)] for chip in members], axis=1)
    return lax.dot_general(
        grad_t, projected, (((1,), (1,)), ((), ())), preferred_element_type=jnp.float32
    )


def own_kernel(core_ref, own_ref, grad_t_ref, held_ref, partial_ref, sems):
    tokens = grad_t_ref.shape[1] // CHUNKS
    chips = own_ref.shape[0] // CHUNKS
    copies = []
    for chunk in range(CHUNKS):
        part = pl.ds(chunk * tokens, tokens)
        copies.append(
            pltpu.make_async_copy(grad_t_ref.at[:, part], held_ref.at[:, part], sems.at[chunk])
        )
        copies[-1].start()
    total = jnp.zeros(partial_ref.shape, jnp.float32)
    for chunk in range(CHUNKS):
        copies[chunk].wait()
        total += half_dot(core_ref[0], own_ref, held_ref, chunk * chips, chips)
    partial_ref[...] = total


def own_half(core, own, grad_t):
    chips, rank, rows = own.shape
    hidden, tokens = grad_t.shape
    return pl.pallas_call(
        own_kernel,
        in_specs=[
            pl.BlockSpec(memory_space=pltpu.SMEM),
            pl.BlockSpec(memory_space=pltpu.VMEM),
            pl.BlockSpec(memory_space=pltpu.HBM),
        ],
        out_specs=[pl.BlockSpec(memory_space=pltpu.VMEM), pl.BlockSpec(memory_space=pltpu.VMEM)],
        out_shape=[
            jax.ShapeDtypeStruct((hidden, tokens), jnp.bfloat16),
            jax.ShapeDtypeStruct((hidden, rank), jnp.float32),
        ],
        scratch_shapes=[pltpu.SemaphoreType.DMA((CHUNKS,))],
        compiler_params=pltpu.CompilerParams(vmem_limit_bytes=24 * 1024 * 1024),
        cost_estimate=pl.CostEstimate(
            flops=2 * rank * hidden * tokens, bytes_accessed=4 * hidden * tokens, transcendentals=0
        ),
    )(core, own, grad_t)


def moments_kernel(core_ref, other_ref, held_ref, partial_ref, first_ref, second_ref,
                   new_first_ref, new_second_ref, spread_ref, first_in, second_in, sems):
    reads = [
        pltpu.make_async_copy(first_ref, first_in, sems.at[0]),
        pltpu.make_async_copy(second_ref, second_in, sems.at[1]),
    ]
    for read in reads:
        read.start()
    chips = other_ref.shape[0] // PIECES
    total = partial_ref[...]
    for piece in range(PIECES):
        total += half_dot(1 - core_ref[0], other_ref, held_ref, piece * chips, chips)
    for read in reads:
        read.wait()
    new_first, new_second, direction = moments_step(total.T, first_in[...], second_in[...])
    new_first_ref[...] = new_first
    new_second_ref[...] = new_second
    packed = pack(direction)
    for copy in range(spread_ref.shape[0]):
        spread_ref[copy] = packed


def other_half_and_moments(core, other, held, partial, first_moment, second_moment, copies):
    rank, hidden = first_moment.shape
    vmem = pl.BlockSpec(memory_space=pltpu.VMEM)
    hbm = pl.BlockSpec(memory_space=pltpu.HBM)
    return pl.pallas_call(
        moments_kernel,
        in_specs=[pl.BlockSpec(memory_space=pltpu.SMEM), vmem, vmem, vmem, hbm, hbm],
        out_specs=[vmem, vmem, vmem],
        out_shape=[
            jax.ShapeDtypeStruct((rank, hidden), jnp.float32),
            jax.ShapeDtypeStruct((rank, hidden), jnp.float32),
            jax.ShapeDtypeStruct((copies, rank * hidden // LANES, LANES), jnp.bfloat16),
        ],
        scratch_shapes=[
            pltpu.VMEM((rank, hidden), jnp.float32),
            pltpu.VMEM((rank, hidden), jnp.float32),
            pltpu.SemaphoreType.DMA((2,)),
        ],
        compiler_params=pltpu.CompilerParams(vmem_limit_bytes=24 * 1024 * 1024),
    )(core, other, held, partial, first_moment, second_moment)


PARTS = 4


def project_kernel(acts_ref, basis_ref, terms_ref, acts_in, basis_in, sems):
    depth = acts_ref.shape[1] // PARTS
    reads = []
    for part in range(PARTS):
        at = pl.ds(part * depth, depth)
        reads.append(
            (
                pltpu.make_async_copy(acts_ref.at[:, at], acts_in.at[:, at], sems.at[0, part]),
                pltpu.make_async_copy(basis_ref.at[at, :], basis_in.at[at, :], sems.at[1, part]),
            )
        )
        for read in reads[-1]:
            read.start()
    total = jnp.zeros((acts_ref.shape[0], basis_ref.shape[1]), jnp.float32)
    for part in range(PARTS):
        for read in reads[part]:
            read.wait()
        at = pl.ds(part * depth, depth)
        total += jnp.dot(acts_in[:, at], basis_in[at, :], preferred_element_type=jnp.float32)
    terms_ref[...] = total.T.astype(jnp.bfloat16)


def project(acts, basis):
    tokens, ranks = acts.shape[0], basis.shape[1]
    hbm = pl.BlockSpec(memory_space=pltpu.HBM)
    return pl.pallas_call(
        project_kernel,
        in_specs=[hbm, hbm],
        out_specs=pl.BlockSpec(memory_space=pltpu.VMEM),
        out_shape=jax.ShapeDtypeStruct((ranks, tokens), jnp.bfloat16),
        scratch_shapes=[
            pltpu.VMEM(acts.shape, jnp.bfloat16),
            pltpu.VMEM(basis.shape, jnp.bfloat16),
            pltpu.SemaphoreType.DMA((2, PARTS)),
        ],
        compiler_params=pltpu.CompilerParams(vmem_limit_bytes=16 * 1024 * 1024),
    )(acts, basis)


def update_kernel(pieces_ref, basis_ref, update_t_ref, strips_ref, sems):
    hidden = update_t_ref.shape[0]
    rank = basis_ref.shape[1] // pieces_ref.shape[0]
    direction = jnp.concatenate(
        [unpack(pieces_ref[split], rank, hidden - LANES) for split in range(pieces_ref.shape[0])], axis=0
    )
    direction_t = direction.T
    width = basis_ref.shape[0] // STRIPS
    writes = []
    for strip in range(STRIPS):
        at = pl.ds(strip * width, width)
        strips_ref[:, at] = lax.dot_general(
            direction_t, basis_ref[at, :], (((1,), (1,)), ((), ())), preferred_element_type=jnp.float32
        )
        writes.append(
            pltpu.make_async_copy(strips_ref.at[:, at], update_t_ref.at[:, at], sems.at[strip])
        )
        writes[-1].start()
    for write in writes:
        write.wait()


def expand(pieces, basis, hidden):
    vmem = pl.BlockSpec(memory_space=pltpu.VMEM)
    return pl.pallas_call(
        update_kernel,
        in_specs=[vmem, vmem],
        out_specs=pl.BlockSpec(memory_space=pltpu.HBM),
        out_shape=jax.ShapeDtypeStruct((hidden, basis.shape[0]), jnp.float32),
        scratch_shapes=[
            pltpu.VMEM((hidden, basis.shape[0]), jnp.float32),
            pltpu.SemaphoreType.DMA((STRIPS,)),
        ],
        compiler_params=pltpu.CompilerParams(vmem_limit_bytes=24 * 1024 * 1024),
    )(pieces, basis)


def per_device(acts, out_grad, basis, first_moment, second_moment):
    splits = lax.axis_size("x")
    chips = lax.axis_size("z") * lax.axis_size("y")
    tokens = acts.shape[0]
    rank = basis.shape[1] // splits
    in_hbm = lambda array: pltpu.with_memory_space_constraint(array, pltpu.HBM)
    grad_t = in_hbm(out_grad.T)
    local_terms = project(in_hbm(acts), in_hbm(basis))
    terms = lax.all_to_all(
        local_terms.reshape(splits, rank, tokens), "x", split_axis=0, concat_axis=0, tiled=True
    )
    spread = sum_and_spread(terms, chips)
    own = lax.all_to_all(spread, ("z", "y"), split_axis=0, concat_axis=0, tiled=True)
    other = lax.ppermute(own, "c", [(0, 1), (1, 0)])
    core = lax.axis_index("c").astype(jnp.int32).reshape(1)
    held, partial = own_half(core, own, grad_t)
    new_first, new_second, direction = other_half_and_moments(
        core, other, held, partial, first_moment, second_moment, splits
    )
    pieces = lax.all_to_all(direction, "x", split_axis=0, concat_axis=0, tiled=True)
    update = expand(pieces, basis, first_moment.shape[1]).T
    return (update, new_first, new_second)


def solution(mesh):
    chips = Mesh(np.asarray(mesh.devices).reshape(8, 8, 8, 2), ("x", "z", "y", "c"))
    fsdp = ("z", "y", "c")
    return jax.shard_map(
        per_device,
        mesh=chips,
        in_specs=(P(fsdp, "x"), P(None, fsdp), P("x", None), P("x", fsdp), P("x", fsdp)),
        out_specs=(P("x", fsdp), P("x", fsdp), P("x", fsdp)),
        check_vma=False,
    )
```

```python
import jax
import jax.numpy as jnp
import numpy as np
from jax import lax
from jax.experimental import pallas as pl
from jax.experimental.pallas import tpu as pltpu
from jax.sharding import Mesh
from jax.sharding import PartitionSpec as P

STEP = 1000


beta_first = 0.9
beta_second = 0.999
adam_epsilon = 1e-08


def moments_step(grad_low, first_moment, second_moment):
    new_first = beta_first * first_moment + (1.0 - beta_first) * grad_low
    new_second = beta_second * second_moment + (1.0 - beta_second) * grad_low * grad_low
    corrected_first = new_first / (1.0 - beta_first**STEP)
    corrected_second = new_second / (1.0 - beta_second**STEP)
    direction = (corrected_first / (jnp.sqrt(corrected_second) + adam_epsilon)).astype(jnp.bfloat16)
    return (new_first, new_second, direction)


CHUNKS = 16
PIECES = 4
LANES = 128
STRIPS = 4


def pack(block):
    rows, tail = block.shape[0], block.shape[1] - LANES
    kept = rows * tail // LANES
    step = rows - kept
    last = [block[kept:, LANES + at : LANES + at + LANES - tail] for at in range(0, tail, LANES - tail)]
    assert len(last) * step == kept
    below = jnp.concatenate([block[:kept, LANES:], jnp.concatenate(last, axis=0)], axis=1)
    return jnp.concatenate([block[:, :LANES], below], axis=0)


def unpack(packed, rows, tail):
    kept = packed.shape[0] - rows
    step = rows - kept
    beside = packed[rows:, tail:]
    last = jnp.concatenate([beside[at : at + step] for at in range(0, kept, step)], axis=1)
    tails = jnp.concatenate([packed[rows:, :tail], last], axis=0)
    return jnp.concatenate([packed[:rows], tails], axis=1)


def spread_kernel(terms_ref, spread_ref):
    total = terms_ref[0].astype(jnp.float32)
    for split in range(1, terms_ref.shape[0]):
        total += terms_ref[split].astype(jnp.float32)
    share = total.astype(jnp.bfloat16)

    @pl.loop(0, spread_ref.shape[0])
    def _(chip):
        spread_ref[chip] = share


def sum_and_spread(terms, copies):
    return pl.pallas_call(
        spread_kernel,
        in_specs=[pl.BlockSpec(memory_space=pltpu.VMEM)],
        out_specs=pl.BlockSpec(memory_space=pltpu.VMEM),
        out_shape=jax.ShapeDtypeStruct((copies,) + terms.shape[1:], jnp.bfloat16),
        compiler_params=pltpu.CompilerParams(vmem_limit_bytes=8 * 1024 * 1024),
    )(terms)


def half_dot(side, projected_ref, grad_t_ref, first_chip, chips):
    rows = projected_ref.shape[2]
    at = lambda chip: pl.ds(pl.multiple_of((2 * chip + side) * rows, rows), rows)
    members = range(first_chip, first_chip + chips)
    projected = jnp.concatenate([projected_ref[chip] for chip in members], axis=1)
    grad_t = jnp.concatenate([grad_t_ref[:, at(chip)] for chip in members], axis=1)
    return lax.dot_general(
        grad_t, projected, (((1,), (1,)), ((), ())), preferred_element_type=jnp.float32
    )


def own_kernel(core_ref, own_ref, grad_t_ref, held_ref, partial_ref, sems):
    tokens = grad_t_ref.shape[1] // CHUNKS
    chips = own_ref.shape[0] // CHUNKS
    copies = []
    for chunk in range(CHUNKS):
        part = pl.ds(chunk * tokens, tokens)
        copies.append(
            pltpu.make_async_copy(grad_t_ref.at[:, part], held_ref.at[:, part], sems.at[chunk])
        )
        copies[-1].start()
    total = jnp.zeros(partial_ref.shape, jnp.float32)
    for chunk in range(CHUNKS):
        copies[chunk].wait()
        total += half_dot(core_ref[0], own_ref, held_ref, chunk * chips, chips)
    partial_ref[...] = total


def own_half(core, own, grad_t):
    chips, rank, rows = own.shape
    hidden, tokens = grad_t.shape
    return pl.pallas_call(
        own_kernel,
        in_specs=[
            pl.BlockSpec(memory_space=pltpu.SMEM),
            pl.BlockSpec(memory_space=pltpu.VMEM),
            pl.BlockSpec(memory_space=pltpu.HBM),
        ],
        out_specs=[pl.BlockSpec(memory_space=pltpu.VMEM), pl.BlockSpec(memory_space=pltpu.VMEM)],
        out_shape=[
            jax.ShapeDtypeStruct((hidden, tokens), jnp.bfloat16),
            jax.ShapeDtypeStruct((hidden, rank), jnp.float32),
        ],
        scratch_shapes=[pltpu.SemaphoreType.DMA((CHUNKS,))],
        compiler_params=pltpu.CompilerParams(vmem_limit_bytes=24 * 1024 * 1024),
        cost_estimate=pl.CostEstimate(
            flops=2 * rank * hidden * tokens, bytes_accessed=4 * hidden * tokens, transcendentals=0
        ),
    )(core, own, grad_t)


def moments_kernel(core_ref, other_ref, held_ref, partial_ref, first_ref, second_ref,
                   new_first_ref, new_second_ref, spread_ref, first_in, second_in, sems):
    reads = [
        pltpu.make_async_copy(first_ref, first_in, sems.at[0]),
        pltpu.make_async_copy(second_ref, second_in, sems.at[1]),
    ]
    for read in reads:
        read.start()
    chips = other_ref.shape[0] // PIECES
    total = partial_ref[...]
    for piece in range(PIECES):
        total += half_dot(1 - core_ref[0], other_ref, held_ref, piece * chips, chips)
    for read in reads:
        read.wait()
    new_first, new_second, direction = moments_step(total.T, first_in[...], second_in[...])
    new_first_ref[...] = new_first
    new_second_ref[...] = new_second
    packed = pack(direction)
    for copy in range(spread_ref.shape[0]):
        spread_ref[copy] = packed


def other_half_and_moments(core, other, held, partial, first_moment, second_moment, copies):
    rank, hidden = first_moment.shape
    vmem = pl.BlockSpec(memory_space=pltpu.VMEM)
    hbm = pl.BlockSpec(memory_space=pltpu.HBM)
    return pl.pallas_call(
        moments_kernel,
        in_specs=[pl.BlockSpec(memory_space=pltpu.SMEM), vmem, vmem, vmem, hbm, hbm],
        out_specs=[vmem, vmem, vmem],
        out_shape=[
            jax.ShapeDtypeStruct((rank, hidden), jnp.float32),
            jax.ShapeDtypeStruct((rank, hidden), jnp.float32),
            jax.ShapeDtypeStruct((copies, rank * hidden // LANES, LANES), jnp.bfloat16),
        ],
        scratch_shapes=[
            pltpu.VMEM((rank, hidden), jnp.float32),
            pltpu.VMEM((rank, hidden), jnp.float32),
            pltpu.SemaphoreType.DMA((2,)),
        ],
        compiler_params=pltpu.CompilerParams(vmem_limit_bytes=24 * 1024 * 1024),
    )(core, other, held, partial, first_moment, second_moment)


PARTS = 4


def project_kernel(acts_ref, basis_ref, terms_ref, acts_in, basis_in, sems):
    depth = acts_ref.shape[1] // PARTS
    reads = []
    for part in range(PARTS):
        at = pl.ds(part * depth, depth)
        reads.append(
            (
                pltpu.make_async_copy(acts_ref.at[:, at], acts_in.at[:, at], sems.at[0, part]),
                pltpu.make_async_copy(basis_ref.at[at, :], basis_in.at[at, :], sems.at[1, part]),
            )
        )
        for read in reads[-1]:
            read.start()
    total = jnp.zeros((acts_ref.shape[0], basis_ref.shape[1]), jnp.float32)
    for part in range(PARTS):
        for read in reads[part]:
            read.wait()
        at = pl.ds(part * depth, depth)
        total += jnp.dot(acts_in[:, at], basis_in[at, :], preferred_element_type=jnp.float32)
    terms_ref[...] = total.T.astype(jnp.bfloat16)


def project(acts, basis):
    tokens, ranks = acts.shape[0], basis.shape[1]
    hbm = pl.BlockSpec(memory_space=pltpu.HBM)
    return pl.pallas_call(
        project_kernel,
        in_specs=[hbm, hbm],
        out_specs=pl.BlockSpec(memory_space=pltpu.VMEM),
        out_shape=jax.ShapeDtypeStruct((ranks, tokens), jnp.bfloat16),
        scratch_shapes=[
            pltpu.VMEM(acts.shape, jnp.bfloat16),
            pltpu.VMEM(basis.shape, jnp.bfloat16),
            pltpu.SemaphoreType.DMA((2, PARTS)),
        ],
        compiler_params=pltpu.CompilerParams(vmem_limit_bytes=16 * 1024 * 1024),
    )(acts, basis)


def update_kernel(pieces_ref, basis_ref, first_ref, second_ref,
                  update_t_ref, new_first_ref, new_second_ref, strips_ref, sems):
    writes = [
        pltpu.make_async_copy(first_ref, new_first_ref, sems.at[STRIPS]),
        pltpu.make_async_copy(second_ref, new_second_ref, sems.at[STRIPS + 1]),
    ]
    for write in writes:
        write.start()
    hidden = update_t_ref.shape[0]
    rank = basis_ref.shape[1] // pieces_ref.shape[0]
    direction = jnp.concatenate(
        [unpack(pieces_ref[split], rank, hidden - LANES) for split in range(pieces_ref.shape[0])], axis=0
    )
    direction_t = direction.T
    width = basis_ref.shape[0] // STRIPS
    for strip in range(STRIPS):
        at = pl.ds(strip * width, width)
        strips_ref[:, at] = lax.dot_general(
            direction_t, basis_ref[at, :], (((1,), (1,)), ((), ())), preferred_element_type=jnp.float32
        )
        writes.append(
            pltpu.make_async_copy(strips_ref.at[:, at], update_t_ref.at[:, at], sems.at[strip])
        )
        writes[-1].start()
    for write in writes:
        write.wait()


def expand(pieces, basis, new_first, new_second):
    hidden = new_first.shape[1]
    vmem = pl.BlockSpec(memory_space=pltpu.VMEM)
    return pl.pallas_call(
        update_kernel,
        in_specs=[vmem, vmem, vmem, vmem],
        out_specs=[pl.BlockSpec(memory_space=pltpu.HBM)] * 3,
        out_shape=[
            jax.ShapeDtypeStruct((hidden, basis.shape[0]), jnp.float32),
            jax.ShapeDtypeStruct(new_first.shape, jnp.float32),
            jax.ShapeDtypeStruct(new_second.shape, jnp.float32),
        ],
        scratch_shapes=[
            pltpu.VMEM((hidden, basis.shape[0]), jnp.float32),
            pltpu.SemaphoreType.DMA((STRIPS + 2,)),
        ],
        compiler_params=pltpu.CompilerParams(vmem_limit_bytes=24 * 1024 * 1024),
    )(pieces, basis, new_first, new_second)


def per_device(acts, out_grad, basis, first_moment, second_moment):
    splits = lax.axis_size("x")
    chips = lax.axis_size("z") * lax.axis_size("y")
    tokens = acts.shape[0]
    rank = basis.shape[1] // splits
    in_hbm = lambda array: pltpu.with_memory_space_constraint(array, pltpu.HBM)
    grad_t = in_hbm(out_grad.T)
    local_terms = project(in_hbm(acts), in_hbm(basis))
    terms = lax.all_to_all(
        local_terms.reshape(splits, rank, tokens), "x", split_axis=0, concat_axis=0, tiled=True
    )
    spread = sum_and_spread(terms, chips)
    own = lax.all_to_all(spread, ("z", "y"), split_axis=0, concat_axis=0, tiled=True)
    other = lax.ppermute(own, "c", [(0, 1), (1, 0)])
    core = lax.axis_index("c").astype(jnp.int32).reshape(1)
    held, partial = own_half(core, own, grad_t)
    new_first, new_second, direction = other_half_and_moments(
        core, other, held, partial, first_moment, second_moment, splits
    )
    pieces = lax.all_to_all(direction, "x", split_axis=0, concat_axis=0, tiled=True)
    update_t, new_first, new_second = expand(pieces, basis, new_first, new_second)
    return (update_t.T, new_first, new_second)


def solution(mesh):
    chips = Mesh(np.asarray(mesh.devices).reshape(8, 8, 8, 2), ("x", "z", "y", "c"))
    fsdp = ("z", "y", "c")
    return jax.shard_map(
        per_device,
        mesh=chips,
        in_specs=(P(fsdp, "x"), P(None, fsdp), P("x", None), P("x", fsdp), P("x", fsdp)),
        out_specs=(P("x", fsdp), P("x", fsdp), P("x", fsdp)),
        check_vma=False,
    )
```
